128 devices in a mesh: section: 2 (over core), rows: 8 (over x, y_lo), cols: 8 (over y_hi, z).
Axes of the slice: x: 4, y: 4 (y_hi: 2, y_lo: 2; y = y_hi * 2 + y_lo), z: 4, core: 2. Of those that a mesh axis runs over, the one named last changes fastest.
Arguments:
- tensor_data: bfloat16 [1024, 16, 32768], P('rows', 'section', 'cols'), may hold values from 0 to 3
- matrix_data: bfloat16 [1024, 32768], P('rows', ('cols', 'section')), may hold values from 0 to 3
- word_factor: bfloat16 [300, 1024], P(None, 'rows'), may hold values from -2.5 to 2.5
- context_factor: bfloat16 [300, 32768], P(None, 'cols'), may hold values from -2.5 to 2.5
- offset_factor: bfloat16 [300, 16], P(None, 'section'), may hold values from -2.5 to 2.5
Outputs:
- grad_word: float32 [300, 1024], P(None, 'rows')
- grad_context: float32 [300, 32768], P(None, ('cols', 'section', 'rows'))
- grad_offset: float32 [300, 16], P(None, 'section')
The draws below stay inside these ranges and needn't reach their ends.
All inputs are finite; a program needn't handle non-finite values.
Results may differ from the reference program's by a relative error of at most 0.0012.
Values sent between devices are 32-bit elements; how exact they have to be, the bound alone decides.
No kernel may reach another device: no remote copies, remote signals or barrier semaphores. Data moves between devices by JAX's collectives and lax.ppermute only.
A program may use at most 256 MiB of HBM per device.

```python
import math
import jax
import jax.numpy as jnp
from jax import lax

H = 1024
J = 32768
K = 16
R = 300


def block_levels(rng, extent, pieces, smallest, top_value):
    level = 1.0
    for position, blocks in pieces:
        draws = jax.random.uniform(jax.random.fold_in(jax.random.fold_in(rng, 6), position), (blocks,), jnp.float32, smallest / len(pieces), top_value / len(pieces))
        level = level * jnp.repeat(jnp.exp(draws), extent[position] // blocks).reshape((-1,) + (1,) * (len(extent) - 1 - position))
    return level


def gaussian(rng, extent, spread, most, split=(), kind=jnp.bfloat16):
    loudness = block_levels(rng, extent, split, -0.22, 0.18) if split else 1.0
    values = jax.random.normal(rng, extent, jnp.float32) * spread * loudness
    return jnp.minimum(jnp.maximum(values, -most), most).astype(kind)


def setup_inputs(seed: int = 0) -> dict:
    seeds = jax.random.split(jax.random.key(seed), 6)
    tensor_data = jnp.clip(3.0 * jax.random.uniform(seeds[0], (H, K, J), jnp.float32) ** block_levels(seeds[0], (H, K, J), ((0, 8), (1, 2), (2, 8)), -0.2, 0.2), 0.0, 3.0).astype(jnp.bfloat16)
    matrix_data = jnp.clip(3.0 * jax.random.uniform(seeds[1], (H, J), jnp.float32) ** block_levels(seeds[1], (H, J), ((0, 8), (1, 16)), -0.2, 0.2), 0.0, 3.0).astype(jnp.bfloat16)
    word_factor = gaussian(seeds[2], (R, H), 0.4, 2.5, ((1, 8),))
    context_factor = gaussian(seeds[3], (R, J), 0.4, 2.5, ((1, 8),))
    offset_factor = gaussian(seeds[4], (R, K), 0.4, 2.5, ((1, 2),))
    return {"tensor_data": tensor_data, "matrix_data": matrix_data, "word_factor": word_factor, "context_factor": context_factor, "offset_factor": offset_factor}


def contract_first(left, right):
    return lax.dot_general(left, right, (((0,), (0,)), ((), ())), preferred_element_type=jnp.float32)

def contract_last(left, right):
    return lax.dot_general(left, right, (((1,), (1,)), ((), ())), preferred_element_type=jnp.float32)

def reference(tensor_data, matrix_data, word_factor, context_factor, offset_factor):
    offset_wide = offset_factor.astype(jnp.float32)
    context_wide = context_factor.astype(jnp.float32)
    paired = (offset_wide[:, :, None] * context_wide[:, None, :]).astype(jnp.bfloat16).reshape(R, K * J)
    unfolded = tensor_data.reshape(H, K * J)
    block_rows = math.gcd(H, 128)

    def per_block(totals, block_index):
        begin_row = block_index * block_rows
        slab_rows = lax.dynamic_slice_in_dim(unfolded, begin_row, block_rows, 0)
        slab_words = lax.dynamic_slice_in_dim(word_factor, begin_row, block_rows, 1)
        fitted = contract_first(slab_words, paired)
        residual = (fitted - slab_rows.astype(jnp.float32)).astype(jnp.bfloat16)
        word_part = contract_last(paired, residual)
        weighted = jnp.dot(slab_words, residual, preferred_element_type=jnp.float32).reshape(R, K, J)
        context_total = totals[0] + lax.optimization_barrier(jnp.sum(weighted * offset_wide[:, :, None], axis=1))
        offset_total = totals[1] + lax.optimization_barrier(jnp.sum(weighted * context_wide[:, None, :], axis=2))
        return ((context_total, offset_total), word_part)
    start_totals = (jnp.zeros((R, J), jnp.float32), jnp.zeros((R, K), jnp.float32))
    totals, word_parts = lax.scan(per_block, start_totals, jnp.arange(H // block_rows, dtype=jnp.int32))
    context_tensor, offset_total = totals
    word_tensor = jnp.transpose(word_parts, (1, 0, 2)).reshape(R, H)
    fitted_matrix = contract_first(word_factor, context_factor)
    residual_matrix = (fitted_matrix - matrix_data.astype(jnp.float32)).astype(jnp.bfloat16)
    word_matrix = contract_last(context_factor, residual_matrix)
    context_matrix = jnp.dot(word_factor, residual_matrix, preferred_element_type=jnp.float32)
    grad_word = (word_tensor + word_matrix) / math.sqrt(J * K)
    grad_context = (context_tensor + context_matrix) / math.sqrt(H * K)
    grad_offset = offset_total / math.sqrt(H * J)
    return (grad_word, grad_context, grad_offset)
```

```python
import functools
import math

import jax
import jax.numpy as jnp
from jax import lax
from jax.experimental import pallas as pl
from jax.experimental.pallas import tpu as pltpu
from jax.sharding import PartitionSpec as P

F32 = jnp.float32
BF16 = jnp.bfloat16
MIB = 1024 * 1024
NT = (((1,), (1,)), ((), ()))
TN = (((0,), (0,)), ((), ()))


def dot(a, b):
    return jnp.dot(a, b, preferred_element_type=F32)


def dot_nt(a, b):
    return lax.dot_general(a, b, NT, preferred_element_type=F32)


def dot_tn(a, b):
    return lax.dot_general(a, b, TN, preferred_element_type=F32)


def split_two(v):
    hi = v.astype(BF16)
    return hi, (v - hi.astype(F32)).astype(BF16)


def word_spread(words, offsets):
    n = words * offsets
    col = lax.broadcasted_iota(jnp.int32, (words, n), 1)
    row = lax.broadcasted_iota(jnp.int32, (words, n), 0)
    inside = (col >= row * offsets) & (col < row * offsets + offsets)
    return jnp.where(inside, 1.0, 0.0).astype(BF16)


def offset_spread(words, offsets):
    n = words * offsets
    col = lax.broadcasted_iota(jnp.int32, (offsets, n), 1)
    row = lax.broadcasted_iota(jnp.int32, (offsets, n), 0)
    return jnp.where(lax.rem(col, offsets) == row, 1.0, 0.0).astype(BF16)


def context_kernel(own, pos_ref, word_ref, off_ref, data_ref, ctx_ref, mat_ref, out_ref, a_ref, hi_ref, lo_ref):
    words, offsets = word_ref.shape[1], off_ref.shape[0]

    @pl.when(pl.program_id(0) == 0)
    def _():
        w = word_ref[...]
        o = off_ref[...]
        wide_w = dot(w, word_spread(words, offsets))
        wide_o = dot_tn(o, offset_spread(words, offsets))
        a_ref[...] = (wide_w * wide_o).astype(BF16)
        gram = dot_tn(o, o)
        if own:
            gram = gram + 1.0
        hi, lo = split_two(dot_nt(w, w) * gram)
        hi_ref[...] = hi
        lo_ref[...] = lo

    c = ctx_ref[...]
    acc = dot(hi_ref[...], c) + dot(lo_ref[...], c) - dot(a_ref[...], data_ref[...])
    if own:
        acc = acc - dot(word_ref[...], mat_ref[...])
    out_ref[...] = acc


def context_part(own, pos, data, matrix, word, off_t, ctx):
    rank, words = word.shape
    offsets = off_t.shape[0]
    rows, width = data.shape
    half = width // 2
    tile = 512
    steps = half // tile

    def column(i, pos):
        which = pos[0] if own else 1 - pos[0]
        return (0, which * steps + i)

    grid_spec = pltpu.PrefetchScalarGridSpec(
        num_scalar_prefetch=1,
        grid=(steps,),
        in_specs=[
            pl.BlockSpec((rank, words), lambda i, pos: (0, 0)),
            pl.BlockSpec((offsets, rank), lambda i, pos: (0, 0)),
            pl.BlockSpec((rows, tile), column),
            pl.BlockSpec((rank, tile), column),
            pl.BlockSpec((words, tile), (lambda i, pos: (0, i)) if own else (lambda i, pos: (0, 0))),
        ],
        out_specs=pl.BlockSpec((rank, tile), lambda i, pos: (0, i)),
        scratch_shapes=[
            pltpu.VMEM((rank, rows), BF16),
            pltpu.VMEM((rank, rank), BF16),
            pltpu.VMEM((rank, rank), BF16),
        ],
    )
    flops = 2 * rank * half * (rows + 2 * rank)
    return pl.pallas_call(
        functools.partial(context_kernel, own),
        out_shape=jax.ShapeDtypeStruct((rank, half), F32),
        grid_spec=grid_spec,
        compiler_params=pltpu.CompilerParams(vmem_limit_bytes=24 * MIB),
        cost_estimate=pl.CostEstimate(flops=flops, bytes_accessed=rows * half * 2 + rank * half * 6, transcendentals=0),
        name="context_own" if own else "context_other",
    )(pos, word, off_t, data, ctx, matrix)


def word_kernel(pos_ref, word_ref, off_ref, data_ref, ctx_ref, mat_ref, word_out, off_out, b_ref, m_ref, c0_ref, c1_ref):
    i = pl.program_id(0)
    steps = pl.num_programs(0)
    words, offsets = word_ref.shape[1], off_ref.shape[0]
    rank = word_ref.shape[0]
    section = pos_ref[0]

    @pl.when(i == 0)
    def _():
        b_ref[...] = jnp.zeros_like(b_ref)
        m_ref[...] = jnp.zeros_like(m_ref)
        c0_ref[...] = jnp.zeros_like(c0_ref)
        c1_ref[...] = jnp.zeros_like(c1_ref)

    c = ctx_ref[...]
    b_ref[...] += dot_nt(c, data_ref[...])
    gram = dot_nt(c, c)
    mine = (i >= section * (steps // 2)) & (i < (section + 1) * (steps // 2))

    @pl.when(mine)
    def _():
        m_ref[...] += dot_nt(c, mat_ref[...])
        c0_ref[...] += gram

    @pl.when(jnp.logical_not(mine))
    def _():
        c1_ref[...] += gram

    @pl.when(i == steps - 1)
    def _():
        w = word_ref[...]
        o = off_ref[...]
        spread_w = word_spread(words, offsets)
        spread_o = offset_spread(words, offsets)
        b = b_ref[...]
        own = c0_ref[...]
        both = own + c1_ref[...]
        n_hi, n_lo = split_two(dot_tn(o, o) * both + own)
        b_hi, b_lo = split_two(b * dot_tn(o, spread_o))
        total = dot(n_hi, w) + dot(n_lo, w) - m_ref[...]
        total = total - dot_nt(b_hi, spread_w) - dot_nt(b_lo, spread_w)
        word_out[...] = jnp.zeros_like(word_out)
        word_out[pl.ds(0, rank), :] = total
        p_hi, p_lo = split_two(dot_nt(w, w) * both)
        v_hi, v_lo = split_two(b * dot(w, spread_w))
        off = dot(o, p_hi) + dot(o, p_lo) - dot_nt(spread_o, v_hi) - dot_nt(spread_o, v_lo)
        off_out[...] = jnp.zeros_like(off_out)
        for k in range(off_out.shape[0] // offsets):
            lanes = min(128, rank - k * 128)
            off_out[pl.ds(k * offsets, offsets), pl.ds(0, lanes)] = off[:, k * 128 : k * 128 + lanes]


def word_part(pos, data, matrix, word, off_t, ctx):
    rank, words = word.shape
    offsets = off_t.shape[0]
    rows, width = data.shape
    tile = 512
    steps = width // tile
    padded = -(-rank // 16) * 16
    chunks = -(-rank // 128)

    def mat_column(i, pos):
        return (0, jnp.clip(i - pos[0] * (steps // 2), 0, steps // 2 - 1))

    grid_spec = pltpu.PrefetchScalarGridSpec(
        num_scalar_prefetch=1,
        grid=(steps,),
        in_specs=[
            pl.BlockSpec((rank, words), lambda i, pos: (0, 0)),
            pl.BlockSpec((offsets, rank), lambda i, pos: (0, 0)),
            pl.BlockSpec((rows, tile), lambda i, pos: (0, i)),
            pl.BlockSpec((rank, tile), lambda i, pos: (0, i)),
            pl.BlockSpec((words, tile), mat_column),
        ],
        out_specs=[
            pl.BlockSpec((padded, words), lambda i, pos: (0, 0)),
            pl.BlockSpec((chunks * offsets, 128), lambda i, pos: (0, 0)),
        ],
        scratch_shapes=[
            pltpu.VMEM((rank, rows), F32),
            pltpu.VMEM((rank, words), F32),
            pltpu.VMEM((rank, rank), F32),
            pltpu.VMEM((rank, rank), F32),
        ],
    )
    return pl.pallas_call(
        word_kernel,
        out_shape=[
            jax.ShapeDtypeStruct((padded, words), F32),
            jax.ShapeDtypeStruct((chunks * offsets, 128), F32),
        ],
        grid_spec=grid_spec,
        compiler_params=pltpu.CompilerParams(vmem_limit_bytes=24 * MIB),
        cost_estimate=pl.CostEstimate(
            flops=2 * rank * width * (rows + rank), bytes_accessed=rows * width * 2 + rank * width * 2, transcendentals=0
        ),
        name="word_offset",
    )(pos, word, off_t, data, ctx, matrix)


def whole_call(kernel, outs, name, pos, *args):
    vmem = pl.BlockSpec(memory_space=pltpu.VMEM)
    total = sum(a.size for a in args) * 4 + sum(math.prod(o) for o in outs) * 4
    return pl.pallas_call(
        kernel,
        out_shape=[jax.ShapeDtypeStruct(o, F32) for o in outs],
        in_specs=[pl.BlockSpec(memory_space=pltpu.SMEM)] + [vmem] * len(args),
        out_specs=[vmem] * len(outs),
        compiler_params=pltpu.CompilerParams(vmem_limit_bytes=24 * MIB),
        cost_estimate=pl.CostEstimate(flops=total // 4, bytes_accessed=total, transcendentals=0),
        name=name,
    )(pos, *args)


def lanes(start, width):
    return pl.ds(pl.multiple_of(start, 128), width)


def first_sum(top, pos_ref, own_ref, got_ref, x1_ref, x2_ref, x3_ref, y_ref, kx_ref, ky_ref):
    x, y = pos_ref[1], pos_ref[2]
    rank = own_ref.shape[0]
    block = ky_ref.shape[1] // 4
    upper, lower = pl.ds(0, top), pl.ds(top, rank - top)
    for hop, ref in ((1, x1_ref), (2, x2_ref), (3, x3_ref), (0, kx_ref)):
        at = lanes(lax.rem(x + hop, 4) * (2 * block), 2 * block)
        ref[...] = own_ref[upper, at] + got_ref[upper, at]
    for side, ref in ((1 - y, y_ref), (y, ky_ref)):
        for k in range(4):
            at = lanes((2 * k + side) * block, block)
            ref[:, pl.ds(k * block, block)] = own_ref[lower, at] + got_ref[lower, at]


def x_sum(pos_ref, k_ref, a_ref, b_ref, c_ref, send_ref, keep_ref):
    y = pos_ref[2]
    block = send_ref.shape[1]
    for side, ref in ((1 - y, send_ref), (y, keep_ref)):
        at = lanes(side * block, block)
        ref[...] = (k_ref[:, at] + a_ref[:, at]) + (b_ref[:, at] + c_ref[:, at])


def y_sum(pos_ref, k_ref, a_ref, x1_ref, x2_ref, x3_ref, keep_ref):
    x = pos_ref[1]
    block = keep_ref.shape[1]
    for hop, ref in ((1, x1_ref), (2, x2_ref), (3, x3_ref), (0, keep_ref)):
        at = lanes(lax.rem(x + hop, 4) * block, block)
        ref[...] = k_ref[:, at] + a_ref[:, at]


def last_sum(scale, pos_ref, k_ref, a_ref, l_ref, b_ref, c_ref, d_ref, out_ref):
    top = k_ref.shape[0]
    rank = out_ref.shape[0]
    out_ref[pl.ds(0, top), :] = (k_ref[...] + a_ref[...]) * scale
    out_ref[pl.ds(top, rank - top), :] = ((l_ref[...] + b_ref[...]) + (c_ref[...] + d_ref[...])) * scale


def rows_perm(move):
    pairs = []
    for x in range(4):
        for y in range(2):
            nx, ny = move(x, y)
            pairs.append((x * 2 + y, (nx % 4) * 2 + ny % 2))
    return pairs


def cols_perm(move):
    pairs = []
    for y in range(2):
        for z in range(4):
            ny, nz = move(y, z)
            pairs.append((y * 4 + z, (ny % 2) * 4 + nz % 4))
    return pairs


X_HOP = {h: rows_perm(lambda x, y, h=h: (x + h, y)) for h in (1, 2, 3)}
Y_LOW = rows_perm(lambda x, y: (x, 1 - y))
Z_HOP = {h: cols_perm(lambda y, z, h=h: (y, z + h)) for h in (1, 2, 3)}
Y_HIGH = cols_perm(lambda y, z: (1 - y, z))
SWAP = [(0, 1), (1, 0)]


def send(v, axis, perm):
    return lax.ppermute(v, axis, perm)


def ring_sum(v, axis, hops):
    a, b, c = (send(v, axis, hops[h]) for h in (1, 2, 3))
    return (v + b) + (a + c)


def per_device(tensor_data, matrix_data, word_factor, context_factor, offset_factor):
    words, offsets, width = tensor_data.shape
    rank = word_factor.shape[0]
    all_words = words * lax.axis_size("rows")
    all_offsets = offsets * lax.axis_size("section")
    all_contexts = width * lax.axis_size("cols")
    section = lax.axis_index("section")
    row = lax.axis_index("rows")
    pos = jnp.stack([section, row // 2, row % 2]).astype(jnp.int32)
    data = tensor_data.reshape(words * offsets, width)
    off_t = offset_factor.T
    args = (pos, data, matrix_data, word_factor, off_t, context_factor)

    other = context_part(False, *args)
    got = send(other, "section", SWAP)
    own = context_part(True, *args)

    top = -(-rank // 16) * 8
    low = rank - top
    block = width // 16
    x1, x2, x3, y1, kx, ky = whole_call(
        functools.partial(first_sum, top),
        [(top, 2 * block)] * 3 + [(low, 4 * block), (top, 2 * block), (low, 4 * block)],
        "first_sum", pos, own, got,
    )
    f2 = send(x2, "rows", X_HOP[2])
    f1 = send(x1, "rows", X_HOP[1])
    f3 = send(x3, "rows", X_HOP[3])
    g = send(y1, "rows", Y_LOW)
    sx, kx = whole_call(x_sum, [(top, block)] * 2, "x_sum", pos, kx, f1, f2, f3)
    x1, x2, x3, ky = whole_call(y_sum, [(low, block)] * 4, "y_sum", pos, ky, g)
    f2 = send(x2, "rows", X_HOP[2])
    f1 = send(x1, "rows", X_HOP[1])
    f3 = send(x3, "rows", X_HOP[3])
    g = send(sx, "rows", Y_LOW)
    scale = 1.0 / math.sqrt(all_words * all_offsets)
    (grad_context,) = whole_call(
        functools.partial(last_sum, scale), [(rank, block)], "last_sum", pos, kx, g, ky, f1, f2, f3
    )

    word_own, off_own = word_part(*args)
    part = word_own.shape[0] // 2
    away = lax.dynamic_slice_in_dim(word_own, (1 - section) * part, part, 0)
    home = lax.dynamic_slice_in_dim(word_own, section * part, part, 0)
    home = home + send(away, "section", SWAP)
    both = jnp.concatenate([home, off_own], axis=0)
    both = ring_sum(both, "cols", Z_HOP)
    both = both + send(both, "cols", Y_HIGH)
    home = both[:part]
    away = send(home, "section", SWAP)
    first = jnp.where(section == 0, home, away)
    second = jnp.where(section == 0, away, home)
    grad_word = jnp.concatenate([first, second], axis=0)[:rank] / math.sqrt(all_contexts * all_offsets)
    off = ring_sum(both[part:], "rows", X_HOP)
    off = off + send(off, "rows", Y_LOW)
    off = jnp.concatenate([off[k * offsets : (k + 1) * offsets] for k in range(off.shape[0] // offsets)], axis=1)
    grad_offset = (off[:, :rank] / math.sqrt(all_words * all_contexts)).T
    return (grad_word, grad_context, grad_offset)


def solution(mesh):
    return jax.shard_map(
        per_device,
        mesh=mesh,
        in_specs=(
            P("rows", "section", "cols"),
            P("rows", ("cols", "section")),
            P(None, "rows"),
            P(None, "cols"),
            P(None, "section"),
        ),
        out_specs=(P(None, "rows"), P(None, ("cols", "section", "rows")), P(None, "section")),
        check_vma=False,
    )
```

```python
import functools
import math

import jax
import jax.numpy as jnp
from jax import lax
from jax.experimental import pallas as pl
from jax.experimental.pallas import tpu as pltpu
from jax.sharding import PartitionSpec as P

F32 = jnp.float32
BF16 = jnp.bfloat16
MIB = 1024 * 1024
BIG = 50 * MIB
OWN = 42 * MIB
WORD = 50 * MIB
FRONT_TILE = 512
TOP = 160
NT = (((1,), (1,)), ((), ()))
TN = (((0,), (0,)), ((), ()))


def dot(a, b):
    return jnp.dot(a, b, preferred_element_type=F32)


def dot_nt(a, b):
    return lax.dot_general(a, b, NT, preferred_element_type=F32)


def dot_tn(a, b):
    return lax.dot_general(a, b, TN, preferred_element_type=F32)


def split_two(v):
    hi = v.astype(BF16)
    return hi, (v - hi.astype(F32)).astype(BF16)


def chunk_count(rank):
    return -(-rank // 128)


def word_spread(words, offsets):
    n = words * offsets
    col = lax.broadcasted_iota(jnp.int32, (words, n), 1)
    row = lax.broadcasted_iota(jnp.int32, (words, n), 0)
    inside = (col >= row * offsets) & (col < row * offsets + offsets)
    return jnp.where(inside, 1.0, 0.0).astype(BF16)


def offset_spread(words, offsets):
    n = words * offsets
    col = lax.broadcasted_iota(jnp.int32, (offsets, n), 1)
    row = lax.broadcasted_iota(jnp.int32, (offsets, n), 0)
    return jnp.where(lax.rem(col, offsets) == row, 1.0, 0.0).astype(BF16)


def start_loads(plan):
    steps = []
    for parts in plan:
        copies = [pltpu.make_async_copy(*p) for p in parts]
        for c in copies:
            c.start()
        steps.append(copies)
    return steps


def front_kernel(pos_ref, word_ref, off_ref, data_ref, ctx_ref, mat_ref, *refs):
    ctx_out, a_out, out_ref, d_buf, c_buf, m_buf, d_sem, c_sem, m_sem = refs
    steps, _, tile = d_buf.shape
    words, offsets = word_ref.shape[1], off_ref.shape[0]
    rank = word_ref.shape[0]
    section = pos_ref[0]
    half = steps // 2
    plan = []
    for i in range(steps):
        side = 1 - section if i < half else section
        at = lanes((side * half + i % half) * tile, tile)
        plan.append([(ctx_ref.at[:, at], c_buf.at[i], c_sem.at[i]), (data_ref.at[:, at], d_buf.at[i], d_sem.at[i])])
        if i >= half:
            k = i - half
            plan[-1].append((mat_ref.at[:, pl.ds(k * tile, tile)], m_buf.at[k], m_sem.at[k]))
    loads = start_loads(plan)
    w = word_ref[...]
    o = off_ref[...]
    spread_w = word_spread(words, offsets)
    spread_o = offset_spread(words, offsets)
    wide_w = dot(w, spread_w)
    wide_o = dot_tn(o, spread_o)
    a = (wide_w * wide_o).astype(BF16)
    a_out[...] = a
    gram_w = dot_nt(w, w)
    gram_o = dot_tn(o, o)
    m_hi, m_lo = split_two(gram_w * gram_o)
    b = m = own = other = None

    def plus(total, term):
        return term if total is None else total + term

    for i in range(steps):
        for c in loads[i]:
            c.wait()
        c = c_buf[i]
        gram = dot_nt(c, c)
        if i < half:
            ctx_out[:, pl.ds(i * tile, tile)] = dot(m_hi, c) + dot(m_lo, c) - dot(a, d_buf[i])
            other = plus(other, gram)
        else:
            m = plus(m, dot_nt(c, m_buf[i - half]))
            own = plus(own, gram)
        b = plus(b, dot_nt(c, d_buf[i]))

    both = own + other
    n_hi, n_lo = split_two(gram_o * both + own)
    b_hi, b_lo = split_two(b * wide_o)
    total = dot(n_hi, w) + dot(n_lo, w) - m
    total = total - dot_nt(b_hi, spread_w) - dot_nt(b_lo, spread_w)
    low = out_ref.shape[0] - chunk_count(rank) * offsets
    out_ref[pl.ds(0, rank), :] = total
    out_ref[pl.ds(rank, low - rank), :] = jnp.zeros((low - rank, words), F32)
    p_hi, p_lo = split_two(gram_w * both)
    v_hi, v_lo = split_two(b * wide_w)
    off = dot_nt(p_hi, o) + dot_nt(p_lo, o) - dot_nt(v_hi, spread_o) - dot_nt(v_lo, spread_o)
    off = off.T
    for k in range(chunk_count(rank)):
        part = min(128, rank - k * 128)
        at = pl.ds(low + k * offsets, offsets)
        out_ref[at, :] = jnp.zeros((offsets, 128), F32)
        out_ref[at, pl.ds(0, part)] = off[:, k * 128 : k * 128 + part]


def front_part(pos, data, matrix, word, off_t, ctx):
    rank, words = word.shape
    offsets = off_t.shape[0]
    rows, width = data.shape
    tile = min(FRONT_TILE, width // 2)
    steps = width // tile
    half = steps // 2
    out_rows = -(-rank // 8) * 8 + chunk_count(rank) * offsets
    vmem = pl.BlockSpec(memory_space=pltpu.VMEM)
    anywhere = pl.BlockSpec(memory_space=pl.ANY)
    return pl.pallas_call(
        front_kernel,
        out_shape=[
            jax.ShapeDtypeStruct((rank, width // 2), F32),
            jax.ShapeDtypeStruct((rank, rows), BF16),
            jax.ShapeDtypeStruct((out_rows, words), F32),
        ],
        in_specs=[pl.BlockSpec(memory_space=pltpu.SMEM), vmem, vmem] + [anywhere] * 3,
        out_specs=[vmem] * 3,
        scratch_shapes=[
            pltpu.VMEM((steps, rows, tile), BF16),
            pltpu.VMEM((steps, rank, tile), BF16),
            pltpu.VMEM((half, words, tile), BF16),
            pltpu.SemaphoreType.DMA((steps,)),
            pltpu.SemaphoreType.DMA((steps,)),
            pltpu.SemaphoreType.DMA((half,)),
        ],
        compiler_params=pltpu.CompilerParams(vmem_limit_bytes=WORD),
        cost_estimate=pl.CostEstimate(
            flops=3 * rank * width * (rows + rank), bytes_accessed=rows * width * 2 + rank * width * 2, transcendentals=0
        ),
        name="front",
    )(pos, word, off_t, data, ctx, matrix)


def own_kernel(pos_ref, word_ref, off_ref, a_ref, data_ref, ctx_ref, mat_ref, after_ref, out_ref, *refs):
    del after_ref
    d_buf, c_buf, m_buf, d_sem, c_sem, m_sem = refs
    steps, _, tile = d_buf.shape
    base = pos_ref[0] * (steps * tile)
    plan = []
    for i in range(steps):
        here = pl.ds(i * tile, tile)
        there = lanes(base + i * tile, tile)
        plan.append([
            (ctx_ref.at[:, there], c_buf.at[i], c_sem.at[i]),
            (mat_ref.at[:, here], m_buf.at[i], m_sem.at[i]),
            (data_ref.at[:, there], d_buf.at[i], d_sem.at[i]),
        ])
    loads = start_loads(plan)
    w = word_ref[...]
    o = off_ref[...]
    a = a_ref[...]
    hi, lo = split_two(dot_nt(w, w) * (dot_tn(o, o) + 1.0))
    for i in range(steps):
        for c in loads[i]:
            c.wait()
        total = dot(hi, c_buf[i]) + dot(lo, c_buf[i]) - dot(w, m_buf[i]) - dot(a, d_buf[i])
        out_ref[:, pl.ds(i * tile, tile)] = total


def own_part(pos, data, matrix, word, off_t, ctx, a, after):
    rank, words = word.shape
    rows, width = data.shape
    half = width // 2
    tile = min(512, half)
    steps = half // tile
    vmem = pl.BlockSpec(memory_space=pltpu.VMEM)
    anywhere = pl.BlockSpec(memory_space=pl.ANY)
    flops = 100 * rank * half * (rows + 2 * rank)
    return pl.pallas_call(
        own_kernel,
        out_shape=jax.ShapeDtypeStruct((rank, half), F32),
        in_specs=[pl.BlockSpec(memory_space=pltpu.SMEM), vmem, vmem, vmem] + [anywhere] * 4,
        out_specs=vmem,
        scratch_shapes=[
            pltpu.VMEM((steps, rows, tile), BF16),
            pltpu.VMEM((steps, rank, tile), BF16),
            pltpu.VMEM((steps, words, tile), BF16),
        ]
        + [pltpu.SemaphoreType.DMA((steps,))] * 3,
        compiler_params=pltpu.CompilerParams(vmem_limit_bytes=OWN),
        cost_estimate=pl.CostEstimate(flops=flops, bytes_accessed=rows * half * 100 + rank * half * 300, transcendentals=0),
        name="own_half",
    )(pos, word, off_t, a, data, ctx, matrix, after)


def whole_call(kernel, outs, name, pos, *args, after=()):
    vmem = pl.BlockSpec(memory_space=pltpu.VMEM)
    anywhere = pl.BlockSpec(memory_space=pl.ANY)
    n = 1 + len(args)

    def body(*refs):
        kernel(*refs[:n], *refs[n + len(after) :])

    return pl.pallas_call(
        body,
        out_shape=[jax.ShapeDtypeStruct(o, F32) for o in outs],
        in_specs=[pl.BlockSpec(memory_space=pltpu.SMEM)] + [vmem] * len(args) + [anywhere] * len(after),
        out_specs=[vmem] * len(outs),
        compiler_params=pltpu.CompilerParams(vmem_limit_bytes=24 * MIB),
        cost_estimate=pl.CostEstimate(flops=1024, bytes_accessed=1024, transcendentals=0),
        name=name,
    )(pos, *args, *after)


def lanes(start, width):
    return pl.ds(pl.multiple_of(start, 128), width)


def first_sum(pos_ref, own_ref, got_ref, x1_ref, x2_ref, x3_ref, y_ref, kx_ref, ky_ref):
    x, y = pos_ref[1], pos_ref[2]
    top, width = kx_ref.shape
    low, span = ky_ref.shape
    block = span // 4
    for hop, ref in ((1, x1_ref), (3, x3_ref), (2, x2_ref), (0, kx_ref)):
        at = lanes(lax.rem(x + hop, 4) * width, width)
        ref[...] = own_ref[pl.ds(0, top), at] + got_ref[pl.ds(0, top), at]
    for side, ref in ((1 - y, y_ref), (y, ky_ref)):
        for k in range(4):
            at = lanes((2 * k + side) * block, block)
            ref[:, pl.ds(k * block, block)] = own_ref[pl.ds(top, low), at] + got_ref[pl.ds(top, low), at]


def middle_sum(pos_ref, k_ref, a_ref, b_ref, c_ref, l_ref, g_ref, off_ref, more_ref, *refs):
    sx_ref, kx_ref, x1_ref, x2_ref, x3_ref, ky_ref = refs
    x, y = pos_ref[1], pos_ref[2]
    block = sx_ref.shape[1]
    low = l_ref.shape[0]
    for hop, ref in ((1, x1_ref), (3, x3_ref), (2, x2_ref), (0, ky_ref)):
        at = lanes(lax.rem(x + hop, 4) * block, block)
        ref[pl.ds(0, low), :] = l_ref[:, at] + g_ref[:, at]
    begin = -(-low // 8) * 8
    extra = ky_ref.shape[0] - begin
    total = off_ref[...] + more_ref[...]
    for ref in (x1_ref, x2_ref, x3_ref, ky_ref):
        if begin > low:
            ref[pl.ds(low, begin - low), :] = jnp.zeros((begin - low, block), F32)
        ref[pl.ds(begin, extra), pl.ds(0, 128)] = total
        ref[pl.ds(begin, extra), pl.ds(128, block - 128)] = jnp.zeros((extra, block - 128), F32)
    for side, ref in ((1 - y, sx_ref), (y, kx_ref)):
        at = lanes(side * block, block)
        ref[...] = (k_ref[:, at] + a_ref[:, at]) + (b_ref[:, at] + c_ref[:, at])


def last_sum(scales, pos_ref, k_ref, a_ref, l_ref, b_ref, c_ref, d_ref, w_ref, v_ref, ctx_ref, word_ref, off_ref):
    top = k_ref.shape[0]
    rank = ctx_ref.shape[0]
    low = rank - top
    ctx_ref[pl.ds(0, top), :] = (k_ref[...] + a_ref[...]) * scales[0]
    rows = pl.ds(0, low)
    ctx_ref[pl.ds(top, low), :] = ((l_ref[rows, :] + c_ref[rows, :]) + (b_ref[rows, :] + d_ref[rows, :])) * scales[0]
    word_ref[...] = (w_ref[pl.ds(0, rank), :] + v_ref[pl.ds(0, rank), :]) * scales[1]
    end = -(-low // 8) * 8
    offsets = off_ref.shape[0]
    for k in range(chunk_count(rank)):
        at = pl.ds(end + k * offsets, offsets)
        part = min(128, rank - k * 128)
        total = (l_ref[at, :] + c_ref[at, :]) + (b_ref[at, :] + d_ref[at, :])
        off_ref[:, pl.ds(k * 128, part)] = total[:, :part] * scales[2]


def rows_perm(move):
    pairs = []
    for x in range(4):
        for y in range(2):
            nx, ny = move(x, y)
            pairs.append((x * 2 + y, (nx % 4) * 2 + ny % 2))
    return pairs


def cols_perm(move):
    pairs = []
    for y in range(2):
        for z in range(4):
            ny, nz = move(y, z)
            pairs.append((y * 4 + z, (ny % 2) * 4 + nz % 4))
    return pairs


X_HOP = {h: rows_perm(lambda x, y, h=h: (x + h, y)) for h in (1, 2, 3)}
Y_LOW = rows_perm(lambda x, y: (x, 1 - y))
Z_PAIR = [cols_perm(lambda y, z, h=h: (y, z ^ h)) for h in (1, 2)]
Y_HIGH = cols_perm(lambda y, z: (1 - y, z))
SWAP = [(0, 1), (1, 0)]


def send(v, axis, perm):
    return lax.ppermute(v, axis, perm)


def per_device(tensor_data, matrix_data, word_factor, context_factor, offset_factor):
    words, offsets, width = tensor_data.shape
    rank = word_factor.shape[0]
    all_words = words * lax.axis_size("rows")
    all_offsets = offsets * lax.axis_size("section")
    all_contexts = width * lax.axis_size("cols")
    section = lax.axis_index("section")
    row = lax.axis_index("rows")
    pos = jnp.stack([section, row // 2, row % 2]).astype(jnp.int32)
    data = tensor_data.reshape(words * offsets, width)
    off_t = offset_factor.T
    other, a, part = front_part(pos, data, matrix_data, word_factor, off_t, context_factor)
    got = send(other, "section", SWAP)
    z1 = send(part, "cols", Z_PAIR[0])
    own = own_part(pos, data, matrix_data, word_factor, off_t, context_factor, a, part)
    part = part + z1
    z2 = send(part, "cols", Z_PAIR[1])

    top = TOP
    low = rank - top
    block = width // 16
    extra = chunk_count(rank) * offsets
    x1, x2, x3, y1, kx, ky = whole_call(
        first_sum, [(top, 2 * block)] * 3 + [(low, 4 * block), (top, 2 * block), (low, 4 * block)],
        "first_sum", pos, own, got, after=(part,),
    )
    f1 = send(x1, "rows", X_HOP[1])
    f3 = send(x3, "rows", X_HOP[3])
    g = send(y1, "rows", Y_LOW)
    f2 = send(x2, "rows", X_HOP[2])
    never = row < 0
    part = part + z2
    part = jnp.where(never, f1[:1, :1], part)
    word = part + send(part, "cols", Y_HIGH)
    off = word[word.shape[0] - extra :]
    more = send(off, "rows", Y_LOW)
    longer = (-(-low // 8) * 8 + extra, block)
    sx, kx, x1, x2, x3, ky = whole_call(
        middle_sum, [(top, block)] * 2 + [longer] * 4, "middle_sum", pos, kx, f1, f2, f3, ky, g, off, more
    )
    f1 = send(x1, "rows", X_HOP[1])
    f3 = send(x3, "rows", X_HOP[3])
    f2 = send(x2, "rows", X_HOP[2])
    g = send(sx, "rows", Y_LOW)
    other_word = send(word, "section", SWAP)
    scales = (
        1.0 / math.sqrt(all_words * all_offsets),
        1.0 / math.sqrt(all_contexts * all_offsets),
        1.0 / math.sqrt(all_words * all_contexts),
    )
    grad_context, grad_word, grad_offset = whole_call(
        functools.partial(last_sum, scales),
        [(rank, block), (rank, words), (offsets, rank)],
        "last_sum", pos, kx, g, ky, f1, f2, f3, word, other_word,
    )
    return (grad_word, grad_context, grad_offset.T)


def solution(mesh):
    return jax.shard_map(
        per_device,
        mesh=mesh,
        in_specs=(
            P("rows", "section", "cols"),
            P("rows", ("cols", "section")),
            P(None, "rows"),
            P(None, "cols"),
            P(None, "section"),
        ),
        out_specs=(P(None, "rows"), P(None, ("cols", "section", "rows")), P(None, "section")),
        check_vma=False,
    )
```

```python
import functools
import math

import jax
import jax.numpy as jnp
from jax import lax
from jax.experimental import pallas as pl
from jax.experimental.pallas import tpu as pltpu
from jax.sharding import PartitionSpec as P

F32 = jnp.float32
BF16 = jnp.bfloat16
MIB = 1024 * 1024
BIG = 50 * MIB
OWN = 42 * MIB
WORD = 50 * MIB
FRONT_TILE = 1024
TOP = 128
NT = (((1,), (1,)), ((), ()))
TN = (((0,), (0,)), ((), ()))


def dot(a, b):
    return jnp.dot(a, b, preferred_element_type=F32)


def dot_nt(a, b):
    return lax.dot_general(a, b, NT, preferred_element_type=F32)


def dot_tn(a, b):
    return lax.dot_general(a, b, TN, preferred_element_type=F32)


def split_two(v):
    hi = v.astype(BF16)
    return hi, (v - hi.astype(F32)).astype(BF16)


def split_diagonal(v):
    n = v.shape[0]
    hi = v.astype(BF16)
    row = lax.broadcasted_iota(jnp.int32, (n, n), 0)
    col = lax.broadcasted_iota(jnp.int32, (n, n), 1)
    rest = jnp.where(row == col, v - hi.astype(F32), 0.0)
    return hi, jnp.sum(rest, axis=1, keepdims=True)


def square(parts):
    left, corner = parts
    right = jnp.concatenate([left[left.shape[1] :].T, corner], axis=0)
    return jnp.concatenate([left, right], axis=1)


def chunk_count(rank):
    return -(-rank // 128)


def word_spread(words, offsets):
    n = words * offsets
    col = lax.broadcasted_iota(jnp.int32, (words, n), 1)
    row = lax.broadcasted_iota(jnp.int32, (words, n), 0)
    inside = (col >= row * offsets) & (col < row * offsets + offsets)
    return jnp.where(inside, 1.0, 0.0).astype(BF16)


def offset_spread(words, offsets):
    n = words * offsets
    col = lax.broadcasted_iota(jnp.int32, (offsets, n), 1)
    row = lax.broadcasted_iota(jnp.int32, (offsets, n), 0)
    return jnp.where(lax.rem(col, offsets) == row, 1.0, 0.0).astype(BF16)


def start_loads(plan):
    steps = []
    for parts in plan:
        copies = [pltpu.make_async_copy(*p) for p in parts]
        for c in copies:
            c.start()
        steps.append(copies)
    return steps


def front_kernel(pos_ref, word_ref, off_ref, data_ref, ctx_ref, mat_ref, *refs):
    ctx_out, a_out, out_ref, d_buf, c_buf, m_buf, d_sem, c_sem, m_sem = refs
    steps, _, tile = d_buf.shape
    words, offsets = word_ref.shape[1], off_ref.shape[0]
    rank = word_ref.shape[0]
    section = pos_ref[0]
    half = steps // 2
    plan = []
    for i in range(steps):
        side = 1 - section if i < half else section
        at = lanes((side * half + i % half) * tile, tile)
        plan.append([(ctx_ref.at[:, at], c_buf.at[i], c_sem.at[i]), (data_ref.at[:, at], d_buf.at[i], d_sem.at[i])])
        if i >= half:
            k = i - half
            plan[-1].append((mat_ref.at[:, pl.ds(k * tile, tile)], m_buf.at[k], m_sem.at[k]))
    loads = start_loads(plan)
    w = word_ref[...]
    o = off_ref[...]
    spread_w = word_spread(words, offsets)
    spread_o = offset_spread(words, offsets)
    wide_w = dot(w, spread_w)
    wide_o = dot_tn(o, spread_o)
    a = (wide_w * wide_o).astype(BF16)
    a_out[...] = a
    gram_w = dot_nt(w, w)
    gram_o = dot_tn(o, o)
    m_hi, m_rest = split_diagonal(gram_w * gram_o)
    b = m = own = other = None

    def plus(total, term):
        if total is None:
            return term
        if isinstance(term, tuple):
            return tuple(t + u for t, u in zip(total, term))
        return total + term

    for i in range(steps):
        for c in loads[i]:
            c.wait()
        c = c_buf[i]
        gram = (dot_nt(c, c[:256]), dot_nt(c[256:], c[256:]))
        if i < half:
            ctx_out[:, pl.ds(i * tile, tile)] = dot(m_hi, c) - dot(a, d_buf[i]) + m_rest * c.astype(F32)
            other = plus(other, gram)
        else:
            m = plus(m, dot_nt(c, m_buf[i - half]))
            own = plus(own, gram)
        b = plus(b, dot_nt(c, d_buf[i]))

    own = square(own)
    both = own + square(other)
    n_hi, n_lo = split_two(gram_o * both + own)
    b_hi, b_lo = split_two(b * wide_o)
    total = dot(n_hi, w) + dot(n_lo, w) - m
    total = total - dot_nt(b_hi, spread_w) - dot_nt(b_lo, spread_w)
    low = out_ref.shape[0] - chunk_count(rank) * offsets
    out_ref[pl.ds(0, rank), :] = total
    out_ref[pl.ds(rank, low - rank), :] = jnp.zeros((low - rank, words), F32)
    p_hi, p_lo = split_two(gram_w * both)
    v_hi, v_lo = split_two(b * wide_w)
    off = dot_nt(p_hi, o) + dot_nt(p_lo, o) - dot_nt(v_hi, spread_o) - dot_nt(v_lo, spread_o)
    off = off.T
    for k in range(chunk_count(rank)):
        part = min(128, rank - k * 128)
        at = pl.ds(low + k * offsets, offsets)
        out_ref[at, :] = jnp.zeros((offsets, 128), F32)
        out_ref[at, pl.ds(0, part)] = off[:, k * 128 : k * 128 + part]


def front_part(pos, data, matrix, word, off_t, ctx):
    rank, words = word.shape
    offsets = off_t.shape[0]
    rows, width = data.shape
    tile = min(FRONT_TILE, width // 2)
    steps = width // tile
    half = steps // 2
    out_rows = -(-rank // 8) * 8 + chunk_count(rank) * offsets
    vmem = pl.BlockSpec(memory_space=pltpu.VMEM)
    anywhere = pl.BlockSpec(memory_space=pl.ANY)
    return pl.pallas_call(
        front_kernel,
        out_shape=[
            jax.ShapeDtypeStruct((rank, width // 2), F32),
            jax.ShapeDtypeStruct((rank, rows), BF16),
            jax.ShapeDtypeStruct((out_rows, words), F32),
        ],
        in_specs=[pl.BlockSpec(memory_space=pltpu.SMEM), vmem, vmem] + [anywhere] * 3,
        out_specs=[vmem] * 3,
        scratch_shapes=[
            pltpu.VMEM((steps, rows, tile), BF16),
            pltpu.VMEM((steps, rank, tile), BF16),
            pltpu.VMEM((half, words, tile), BF16),
            pltpu.SemaphoreType.DMA((steps,)),
            pltpu.SemaphoreType.DMA((steps,)),
            pltpu.SemaphoreType.DMA((half,)),
        ],
        compiler_params=pltpu.CompilerParams(vmem_limit_bytes=WORD),
        cost_estimate=pl.CostEstimate(
            flops=3 * rank * width * (rows + rank), bytes_accessed=rows * width * 2 + rank * width * 2, transcendentals=0
        ),
        name="front",
    )(pos, word, off_t, data, ctx, matrix)


def own_kernel(pos_ref, word_ref, off_ref, a_ref, data_ref, ctx_ref, mat_ref, after_ref, out_ref, *refs):
    del after_ref
    d_buf, c_buf, m_buf, d_sem, c_sem, m_sem = refs
    steps, _, tile = d_buf.shape
    base = pos_ref[0] * (steps * tile)
    plan = []
    for i in range(steps):
        here = pl.ds(i * tile, tile)
        there = lanes(base + i * tile, tile)
        plan.append([
            (ctx_ref.at[:, there], c_buf.at[i], c_sem.at[i]),
            (mat_ref.at[:, here], m_buf.at[i], m_sem.at[i]),
            (data_ref.at[:, there], d_buf.at[i], d_sem.at[i]),
        ])
    loads = start_loads(plan)
    w = word_ref[...]
    o = off_ref[...]
    a = a_ref[...]
    hi, rest = split_diagonal(dot_nt(w, w) * (dot_tn(o, o) + 1.0))
    for i in range(steps):
        for c in loads[i]:
            c.wait()
        c = c_buf[i]
        total = dot(hi, c) - dot(w, m_buf[i]) - dot(a, d_buf[i]) + rest * c.astype(F32)
        out_ref[:, pl.ds(i * tile, tile)] = total


def own_part(pos, data, matrix, word, off_t, ctx, a, after):
    rank, words = word.shape
    rows, width = data.shape
    half = width // 2
    tile = min(512, half)
    steps = half // tile
    vmem = pl.BlockSpec(memory_space=pltpu.VMEM)
    anywhere = pl.BlockSpec(memory_space=pl.ANY)
    flops = 100 * rank * half * (rows + 2 * rank)
    return pl.pallas_call(
        own_kernel,
        out_shape=jax.ShapeDtypeStruct((rank, half), F32),
        in_specs=[pl.BlockSpec(memory_space=pltpu.SMEM), vmem, vmem, vmem] + [anywhere] * 4,
        out_specs=vmem,
        scratch_shapes=[
            pltpu.VMEM((steps, rows, tile), BF16),
            pltpu.VMEM((steps, rank, tile), BF16),
            pltpu.VMEM((steps, words, tile), BF16),
        ]
        + [pltpu.SemaphoreType.DMA((steps,))] * 3,
        compiler_params=pltpu.CompilerParams(vmem_limit_bytes=OWN),
        cost_estimate=pl.CostEstimate(flops=flops, bytes_accessed=rows * half * 100 + rank * half * 300, transcendentals=0),
        name="own_half",
    )(pos, word, off_t, a, data, ctx, matrix, after)


def whole_call(kernel, outs, name, pos, *args, after=()):
    vmem = pl.BlockSpec(memory_space=pltpu.VMEM)
    anywhere = pl.BlockSpec(memory_space=pl.ANY)
    n = 1 + len(args)

    def body(*refs):
        kernel(*refs[:n], *refs[n + len(after) :])

    return pl.pallas_call(
        body,
        out_shape=[jax.ShapeDtypeStruct(o, F32) for o in outs],
        in_specs=[pl.BlockSpec(memory_space=pltpu.SMEM)] + [vmem] * len(args) + [anywhere] * len(after),
        out_specs=[vmem] * len(outs),
        compiler_params=pltpu.CompilerParams(vmem_limit_bytes=24 * MIB),
        cost_estimate=pl.CostEstimate(flops=1024, bytes_accessed=1024, transcendentals=0),
        name=name,
    )(pos, *args, *after)


def lanes(start, width):
    return pl.ds(pl.multiple_of(start, 128), width)


def first_sum(pos_ref, own_ref, got_ref, part_ref, more_ref, x1_ref, x2_ref, x3_ref, y_ref, kx_ref, ky_ref, sum_ref):
    x, y = pos_ref[1], pos_ref[2]
    top, width = kx_ref.shape
    low, span = ky_ref.shape
    block = span // 4
    for hop, ref in ((1, x1_ref), (3, x3_ref), (2, x2_ref), (0, kx_ref)):
        at = lanes(lax.rem(x + hop, 4) * width, width)
        ref[...] = own_ref[pl.ds(0, top), at] + got_ref[pl.ds(0, top), at]
    for side, ref in ((1 - y, y_ref), (y, ky_ref)):
        for k in range(4):
            at = lanes((2 * k + side) * block, block)
            ref[:, pl.ds(k * block, block)] = own_ref[pl.ds(top, low), at] + got_ref[pl.ds(top, low), at]
    sum_ref[...] = part_ref[...] + more_ref[...]


def middle_sum(pos_ref, k_ref, a_ref, b_ref, c_ref, l_ref, g_ref, off_ref, more_ref, *refs):
    sx_ref, kx_ref, x1_ref, x2_ref, x3_ref, ky_ref = refs
    x, y = pos_ref[1], pos_ref[2]
    block = sx_ref.shape[1]
    low = l_ref.shape[0]
    for hop, ref in ((1, x1_ref), (3, x3_ref), (2, x2_ref), (0, ky_ref)):
        at = lanes(lax.rem(x + hop, 4) * block, block)
        ref[pl.ds(0, low), :] = l_ref[:, at] + g_ref[:, at]
    begin = -(-low // 8) * 8
    extra = ky_ref.shape[0] - begin
    total = off_ref[...] + more_ref[...]
    for ref in (x1_ref, x2_ref, x3_ref, ky_ref):
        if begin > low:
            ref[pl.ds(low, begin - low), :] = jnp.zeros((begin - low, block), F32)
        ref[pl.ds(begin, extra), pl.ds(0, 128)] = total
        ref[pl.ds(begin, extra), pl.ds(128, block - 128)] = jnp.zeros((extra, block - 128), F32)
    for side, ref in ((1 - y, sx_ref), (y, kx_ref)):
        at = lanes(side * block, block)
        ref[...] = (k_ref[:, at] + a_ref[:, at]) + (b_ref[:, at] + c_ref[:, at])


def last_sum(scales, pos_ref, k_ref, a_ref, l_ref, b_ref, c_ref, d_ref, w_ref, v_ref, ctx_ref, word_ref, off_ref):
    top = k_ref.shape[0]
    rank = ctx_ref.shape[0]
    low = rank - top
    ctx_ref[pl.ds(0, top), :] = (k_ref[...] + a_ref[...]) * scales[0]
    rows = pl.ds(0, low)
    ctx_ref[pl.ds(top, low), :] = ((l_ref[rows, :] + c_ref[rows, :]) + (b_ref[rows, :] + d_ref[rows, :])) * scales[0]
    word_ref[...] = (w_ref[pl.ds(0, rank), :] + v_ref[pl.ds(0, rank), :]) * scales[1]
    end = -(-low // 8) * 8
    offsets = off_ref.shape[0]
    for k in range(chunk_count(rank)):
        at = pl.ds(end + k * offsets, offsets)
        part = min(128, rank - k * 128)
        total = (l_ref[at, :] + c_ref[at, :]) + (b_ref[at, :] + d_ref[at, :])
        off_ref[:, pl.ds(k * 128, part)] = total[:, :part] * scales[2]


def rows_perm(move):
    pairs = []
    for x in range(4):
        for y in range(2):
            nx, ny = move(x, y)
            pairs.append((x * 2 + y, (nx % 4) * 2 + ny % 2))
    return pairs


def cols_perm(move):
    pairs = []
    for y in range(2):
        for z in range(4):
            ny, nz = move(y, z)
            pairs.append((y * 4 + z, (ny % 2) * 4 + nz % 4))
    return pairs


X_HOP = {h: rows_perm(lambda x, y, h=h: (x + h, y)) for h in (1, 2, 3)}
Y_LOW = rows_perm(lambda x, y: (x, 1 - y))
Z_PAIR = [cols_perm(lambda y, z, h=h: (y, z ^ h)) for h in (1, 2)]
Y_HIGH = cols_perm(lambda y, z: (1 - y, z))
SWAP = [(0, 1), (1, 0)]


def send(v, axis, perm):
    return lax.ppermute(v, axis, perm)


def per_device(tensor_data, matrix_data, word_factor, context_factor, offset_factor):
    words, offsets, width = tensor_data.shape
    rank = word_factor.shape[0]
    all_words = words * lax.axis_size("rows")
    all_offsets = offsets * lax.axis_size("section")
    all_contexts = width * lax.axis_size("cols")
    section = lax.axis_index("section")
    row = lax.axis_index("rows")
    pos = jnp.stack([section, row // 2, row % 2]).astype(jnp.int32)
    data = tensor_data.reshape(words * offsets, width)
    off_t = offset_factor.T
    other, a, part = front_part(pos, data, matrix_data, word_factor, off_t, context_factor)
    got = send(other, "section", SWAP)
    more = send(part, "cols", Y_HIGH)
    own = own_part(pos, data, matrix_data, word_factor, off_t, context_factor, a, part)

    top = TOP
    low = rank - top
    block = width // 16
    extra = chunk_count(rank) * offsets
    x1, x2, x3, y1, kx, ky, part = whole_call(
        first_sum, [(top, 2 * block)] * 3 + [(low, 4 * block), (top, 2 * block), (low, 4 * block), part.shape],
        "first_sum", pos, own, got, part, more,
    )
    f1 = send(x1, "rows", X_HOP[1])
    f3 = send(x3, "rows", X_HOP[3])
    g = send(y1, "rows", Y_LOW)
    f2 = send(x2, "rows", X_HOP[2])
    part = part + send(part, "cols", Z_PAIR[0])
    word = part + send(part, "cols", Z_PAIR[1])
    off = word[word.shape[0] - extra :]
    more = send(off, "rows", Y_LOW)
    other_word = send(word, "section", SWAP)
    longer = (-(-low // 8) * 8 + extra, block)
    sx, kx, x1, x2, x3, ky = whole_call(
        middle_sum, [(top, block)] * 2 + [longer] * 4, "middle_sum", pos, kx, f1, f2, f3, ky, g, off, more
    )
    f1 = send(x1, "rows", X_HOP[1])
    f3 = send(x3, "rows", X_HOP[3])
    f2 = send(x2, "rows", X_HOP[2])
    g = send(sx, "rows", Y_LOW)
    scales = (
        1.0 / math.sqrt(all_words * all_offsets),
        1.0 / math.sqrt(all_contexts * all_offsets),
        1.0 / math.sqrt(all_words * all_contexts),
    )
    grad_context, grad_word, grad_offset = whole_call(
        functools.partial(last_sum, scales),
        [(rank, block), (rank, words), (offsets, rank)],
        "last_sum", pos, kx, g, ky, f1, f2, f3, word, other_word,
    )
    return (grad_word, grad_context, grad_offset.T)


def solution(mesh):
    return jax.shard_map(
        per_device,
        mesh=mesh,
        in_specs=(
            P("rows", "section", "cols"),
            P("rows", ("cols", "section")),
            P(None, "rows"),
            P(None, "cols"),
            P(None, "section"),
        ),
        out_specs=(P(None, "rows"), P(None, ("cols", "section", "rows")), P(None, "section")),
        check_vma=False,
    )
```

```python
import functools
import math

import jax
import jax.numpy as jnp
from jax import lax
from jax.experimental import pallas as pl
from jax.experimental.pallas import tpu as pltpu
from jax.sharding import PartitionSpec as P

F32 = jnp.float32
BF16 = jnp.bfloat16
MIB = 1024 * 1024
BIG = 50 * MIB
OWN = 50 * MIB
WORD = 54 * MIB
FRONT_TILE = 1024
TOP = 128
NT = (((1,), (1,)), ((), ()))
TN = (((0,), (0,)), ((), ()))


def dot(a, b):
    return jnp.dot(a, b, preferred_element_type=F32)


def dot_nt(a, b):
    return lax.dot_general(a, b, NT, preferred_element_type=F32)


def dot_tn(a, b):
    return lax.dot_general(a, b, TN, preferred_element_type=F32)


def split_two(v):
    hi = v.astype(BF16)
    return hi, (v - hi.astype(F32)).astype(BF16)


def split_diagonal(v):
    n = v.shape[0]
    hi = v.astype(BF16)
    row = lax.broadcasted_iota(jnp.int32, (n, n), 0)
    col = lax.broadcasted_iota(jnp.int32, (n, n), 1)
    rest = jnp.where(row == col, v - hi.astype(F32), 0.0)
    return hi, jnp.sum(rest, axis=1, keepdims=True)


def square(parts):
    left, corner = parts
    right = jnp.concatenate([left[left.shape[1] :].T, corner], axis=0)
    return jnp.concatenate([left, right], axis=1)


def chunk_count(rank):
    return -(-rank // 128)


def word_spread(words, offsets):
    n = words * offsets
    col = lax.broadcasted_iota(jnp.int32, (words, n), 1)
    row = lax.broadcasted_iota(jnp.int32, (words, n), 0)
    inside = (col >= row * offsets) & (col < row * offsets + offsets)
    return jnp.where(inside, 1.0, 0.0).astype(BF16)


def offset_spread(words, offsets):
    n = words * offsets
    col = lax.broadcasted_iota(jnp.int32, (offsets, n), 1)
    row = lax.broadcasted_iota(jnp.int32, (offsets, n), 0)
    return jnp.where(lax.rem(col, offsets) == row, 1.0, 0.0).astype(BF16)


def start_loads(plan):
    steps = []
    for parts in plan:
        copies = [pltpu.make_async_copy(*p) for p in parts]
        for c in copies:
            c.start()
        steps.append(copies)
    return steps


def position():
    row = lax.axis_index("rows")
    return lax.axis_index("section"), lax.div(row, 2), lax.rem(row, 2)


def front_kernel(pos, word_ref, off_ref, data_ref, ctx_ref, mat_ref, *refs):
    ctx_out, out_ref, d_buf, c_buf, m_buf, d_sem, c_sem, m_sem = refs
    steps, _, tile = d_buf.shape
    words, offsets = word_ref.shape[1], off_ref.shape[0]
    rank = word_ref.shape[0]
    section = pos[0]
    half = steps // 2
    plan = []
    for i in range(steps):
        side = 1 - section if i < half else section
        at = lanes((side * half + i % half) * tile, tile)
        plan.append([(ctx_ref.at[:, at], c_buf.at[i], c_sem.at[i]), (data_ref.at[:, at], d_buf.at[i], d_sem.at[i])])
        if i >= half:
            k = i - half
            plan[-1].append((mat_ref.at[:, pl.ds(k * tile, tile)], m_buf.at[k], m_sem.at[k]))
    loads = start_loads(plan)
    w = word_ref[...]
    o = off_ref[...]
    spread_w = word_spread(words, offsets)
    spread_o = offset_spread(words, offsets)
    wide_w = dot(w, spread_w)
    wide_o = dot_tn(o, spread_o)
    a = (wide_w * wide_o).astype(BF16)
    gram_w = dot_nt(w, w)
    gram_o = dot_tn(o, o)
    m_hi, m_rest = split_diagonal(gram_w * gram_o)
    b = m = own = other = None

    def plus(total, term):
        if total is None:
            return term
        if isinstance(term, tuple):
            return tuple(t + u for t, u in zip(total, term))
        return total + term

    for i in range(steps):
        for c in loads[i]:
            c.wait()
        c = c_buf[i]
        gram = (dot_nt(c, c[:256]), dot_nt(c[256:], c[256:]))
        if i < half:
            ctx_out[:, pl.ds(i * tile, tile)] = dot(m_hi, c) - dot(a, d_buf[i]) + m_rest * c.astype(F32)
            other = plus(other, gram)
        else:
            m = plus(m, dot_nt(c, m_buf[i - half]))
            own = plus(own, gram)
        b = plus(b, dot_nt(c, d_buf[i]))

    own = square(own)
    both = own + square(other)
    n_hi, n_lo = split_two(gram_o * both + own)
    b_hi, b_lo = split_two(b * wide_o)
    total = dot(n_hi, w) + dot(n_lo, w) - m
    total = total - dot_nt(b_hi, spread_w) - dot_nt(b_lo, spread_w)
    low = out_ref.shape[0] - chunk_count(rank) * offsets
    out_ref[pl.ds(0, rank), :] = total
    out_ref[pl.ds(rank, low - rank), :] = jnp.zeros((low - rank, words), F32)
    p_hi, p_lo = split_two(gram_w * both)
    v_hi, v_lo = split_two(b * wide_w)
    off = dot_nt(p_hi, o) + dot_nt(p_lo, o) - dot_nt(v_hi, spread_o) - dot_nt(v_lo, spread_o)
    off = off.T
    for k in range(chunk_count(rank)):
        part = min(128, rank - k * 128)
        at = pl.ds(low + k * offsets, offsets)
        out_ref[at, :] = jnp.zeros((offsets, 128), F32)
        out_ref[at, pl.ds(0, part)] = off[:, k * 128 : k * 128 + part]


def front_part(data, matrix, word, off_t, ctx):
    rank, words = word.shape
    offsets = off_t.shape[0]
    rows, width = data.shape
    tile = min(FRONT_TILE, width // 2)
    steps = width // tile
    half = steps // 2
    out_rows = -(-rank // 8) * 8 + chunk_count(rank) * offsets
    vmem = pl.BlockSpec(memory_space=pltpu.VMEM)
    anywhere = pl.BlockSpec(memory_space=pl.ANY)
    return pl.pallas_call(
        lambda *refs: front_kernel(position(), *refs),
        out_shape=[
            jax.ShapeDtypeStruct((rank, width // 2), F32),
            jax.ShapeDtypeStruct((out_rows, words), F32),
        ],
        in_specs=[vmem, vmem] + [anywhere] * 3,
        out_specs=[vmem] * 2,
        scratch_shapes=[
            pltpu.VMEM((steps, rows, tile), BF16),
            pltpu.VMEM((steps, rank, tile), BF16),
            pltpu.VMEM((half, words, tile), BF16),
            pltpu.SemaphoreType.DMA((steps,)),
            pltpu.SemaphoreType.DMA((steps,)),
            pltpu.SemaphoreType.DMA((half,)),
        ],
        compiler_params=pltpu.CompilerParams(vmem_limit_bytes=WORD),
        cost_estimate=pl.CostEstimate(
            flops=3 * rank * width * (rows + rank), bytes_accessed=rows * width * 2 + rank * width * 2, transcendentals=0
        ),
        name="front",
    )(word, off_t, data, ctx, matrix)


def own_kernel(pos, word_ref, off_ref, data_ref, ctx_ref, mat_ref, after_ref, out_ref, *refs):
    del after_ref
    d_buf, c_buf, m_buf, d_sem, c_sem, m_sem = refs
    steps, _, tile = d_buf.shape
    base = pos[0] * (steps * tile)
    plan = []
    for i in range(steps):
        here = pl.ds(i * tile, tile)
        there = lanes(base + i * tile, tile)
        plan.append([
            (ctx_ref.at[:, there], c_buf.at[i], c_sem.at[i]),
            (mat_ref.at[:, here], m_buf.at[i], m_sem.at[i]),
            (data_ref.at[:, there], d_buf.at[i], d_sem.at[i]),
        ])
    loads = start_loads(plan)
    w = word_ref[...]
    o = off_ref[...]
    words, offsets = w.shape[1], o.shape[0]
    a = (dot(w, word_spread(words, offsets)) * dot_tn(o, offset_spread(words, offsets))).astype(BF16)
    hi, rest = split_diagonal(dot_nt(w, w) * (dot_tn(o, o) + 1.0))
    for i in range(steps):
        for c in loads[i]:
            c.wait()
        c = c_buf[i]
        total = dot(hi, c) - dot(w, m_buf[i]) - dot(a, d_buf[i]) + rest * c.astype(F32)
        out_ref[:, pl.ds(i * tile, tile)] = total


def own_part(data, matrix, word, off_t, ctx, after):
    rank, words = word.shape
    rows, width = data.shape
    half = width // 2
    tile = min(512, half)
    steps = half // tile
    vmem = pl.BlockSpec(memory_space=pltpu.VMEM)
    anywhere = pl.BlockSpec(memory_space=pl.ANY)
    flops = 100 * rank * half * (rows + 2 * rank)
    return pl.pallas_call(
        lambda *refs: own_kernel(position(), *refs),
        out_shape=jax.ShapeDtypeStruct((rank, half), F32),
        in_specs=[vmem, vmem] + [anywhere] * 4,
        out_specs=vmem,
        scratch_shapes=[
            pltpu.VMEM((steps, rows, tile), BF16),
            pltpu.VMEM((steps, rank, tile), BF16),
            pltpu.VMEM((steps, words, tile), BF16),
        ]
        + [pltpu.SemaphoreType.DMA((steps,))] * 3,
        compiler_params=pltpu.CompilerParams(vmem_limit_bytes=OWN),
        cost_estimate=pl.CostEstimate(flops=flops, bytes_accessed=rows * half * 100 + rank * half * 300, transcendentals=0),
        name="own_half",
    )(word, off_t, data, ctx, matrix, after)


def whole_call(kernel, outs, name, *args, after=()):
    vmem = pl.BlockSpec(memory_space=pltpu.VMEM)
    anywhere = pl.BlockSpec(memory_space=pl.ANY)
    n = len(args)

    def body(*refs):
        kernel(position(), *refs[:n], *refs[n + len(after) :])

    return pl.pallas_call(
        body,
        out_shape=[jax.ShapeDtypeStruct(o, F32) for o in outs],
        in_specs=[vmem] * len(args) + [anywhere] * len(after),
        out_specs=[vmem] * len(outs),
        compiler_params=pltpu.CompilerParams(vmem_limit_bytes=24 * MIB),
        cost_estimate=pl.CostEstimate(flops=1024, bytes_accessed=1024, transcendentals=0),
        name=name,
    )(*args, *after)


def lanes(start, width):
    return pl.ds(pl.multiple_of(start, 128), width)


def first_sum(pos, own_ref, got_ref, part_ref, more_ref, x1_ref, x2_ref, x3_ref, y_ref, kx_ref, ky_ref, sum_ref):
    x, y = pos[1], pos[2]
    top, width = kx_ref.shape
    low, span = ky_ref.shape
    block = span // 4
    for hop, ref in ((1, x1_ref), (3, x3_ref), (2, x2_ref), (0, kx_ref)):
        at = lanes(lax.rem(x + hop, 4) * width, width)
        ref[...] = own_ref[pl.ds(0, top), at] + got_ref[pl.ds(0, top), at]
    for side, ref in ((1 - y, y_ref), (y, ky_ref)):
        for k in range(4):
            at = lanes((2 * k + side) * block, block)
            ref[:, pl.ds(k * block, block)] = own_ref[pl.ds(top, low), at] + got_ref[pl.ds(top, low), at]
    sum_ref[...] = part_ref[...] + more_ref[...]


def middle_sum(pos, k_ref, a_ref, b_ref, c_ref, l_ref, g_ref, off_ref, more_ref, *refs):
    sx_ref, kx_ref, x1_ref, x2_ref, x3_ref, ky_ref = refs
    x, y = pos[1], pos[2]
    block = sx_ref.shape[1]
    low = l_ref.shape[0]
    for hop, ref in ((1, x1_ref), (3, x3_ref), (2, x2_ref), (0, ky_ref)):
        at = lanes(lax.rem(x + hop, 4) * block, block)
        ref[pl.ds(0, low), :] = l_ref[:, at] + g_ref[:, at]
    begin = -(-low // 8) * 8
    extra = ky_ref.shape[0] - begin
    total = off_ref[...] + more_ref[...]
    for ref in (x1_ref, x2_ref, x3_ref, ky_ref):
        if begin > low:
            ref[pl.ds(low, begin - low), :] = jnp.zeros((begin - low, block), F32)
        ref[pl.ds(begin, extra), pl.ds(0, 128)] = total
        ref[pl.ds(begin, extra), pl.ds(128, block - 128)] = jnp.zeros((extra, block - 128), F32)
    for side, ref in ((1 - y, sx_ref), (y, kx_ref)):
        at = lanes(side * block, block)
        ref[...] = (k_ref[:, at] + a_ref[:, at]) + (b_ref[:, at] + c_ref[:, at])


def last_sum(scales, pos, k_ref, a_ref, l_ref, b_ref, c_ref, d_ref, w_ref, v_ref, ctx_ref, word_ref, off_ref):
    top = k_ref.shape[0]
    rank = ctx_ref.shape[0]
    low = rank - top
    ctx_ref[pl.ds(0, top), :] = (k_ref[...] + a_ref[...]) * scales[0]
    rows = pl.ds(0, low)
    ctx_ref[pl.ds(top, low), :] = ((l_ref[rows, :] + c_ref[rows, :]) + (b_ref[rows, :] + d_ref[rows, :])) * scales[0]
    word_ref[...] = (w_ref[pl.ds(0, rank), :] + v_ref[pl.ds(0, rank), :]) * scales[1]
    end = -(-low // 8) * 8
    offsets = off_ref.shape[0]
    for k in range(chunk_count(rank)):
        at = pl.ds(end + k * offsets, offsets)
        part = min(128, rank - k * 128)
        total = (l_ref[at, :] + c_ref[at, :]) + (b_ref[at, :] + d_ref[at, :])
        off_ref[:, pl.ds(k * 128, part)] = total[:, :part] * scales[2]


def rows_perm(move):
    pairs = []
    for x in range(4):
        for y in range(2):
            nx, ny = move(x, y)
            pairs.append((x * 2 + y, (nx % 4) * 2 + ny % 2))
    return pairs


def cols_perm(move):
    pairs = []
    for y in range(2):
        for z in range(4):
            ny, nz = move(y, z)
            pairs.append((y * 4 + z, (ny % 2) * 4 + nz % 4))
    return pairs


X_HOP = {h: rows_perm(lambda x, y, h=h: (x + h, y)) for h in (1, 2, 3)}
Y_LOW = rows_perm(lambda x, y: (x, 1 - y))
Z_PAIR = [cols_perm(lambda y, z, h=h: (y, z ^ h)) for h in (1, 2)]
Y_HIGH = cols_perm(lambda y, z: (1 - y, z))
SWAP = [(0, 1), (1, 0)]


def send(v, axis, perm):
    return lax.ppermute(v, axis, perm)


def per_device(tensor_data, matrix_data, word_factor, context_factor, offset_factor):
    words, offsets, width = tensor_data.shape
    rank = word_factor.shape[0]
    all_words = words * lax.axis_size("rows")
    all_offsets = offsets * lax.axis_size("section")
    all_contexts = width * lax.axis_size("cols")
    data = tensor_data.reshape(words * offsets, width)
    off_t = offset_factor.T
    other, part = front_part(data, matrix_data, word_factor, off_t, context_factor)
    got = send(other, "section", SWAP)
    more = send(part, "cols", Y_HIGH)
    own = own_part(data, matrix_data, word_factor, off_t, context_factor, part)

    top = TOP
    low = rank - top
    block = width // 16
    extra = chunk_count(rank) * offsets
    x1, x2, x3, y1, kx, ky, part = whole_call(
        first_sum, [(top, 2 * block)] * 3 + [(low, 4 * block), (top, 2 * block), (low, 4 * block), part.shape],
        "first_sum", own, got, part, more,
    )
    f1 = send(x1, "rows", X_HOP[1])
    f3 = send(x3, "rows", X_HOP[3])
    g = send(y1, "rows", Y_LOW)
    f2 = send(x2, "rows", X_HOP[2])
    part = part + send(part, "cols", Z_PAIR[0])
    word = part + send(part, "cols", Z_PAIR[1])
    off = word[word.shape[0] - extra :]
    more = send(off, "rows", Y_LOW)
    other_word = send(word, "section", SWAP)
    longer = (-(-low // 8) * 8 + extra, block)
    sx, kx, x1, x2, x3, ky = whole_call(
        middle_sum, [(top, block)] * 2 + [longer] * 4, "middle_sum", kx, f1, f2, f3, ky, g, off, more
    )
    f1 = send(x1, "rows", X_HOP[1])
    f3 = send(x3, "rows", X_HOP[3])
    f2 = send(x2, "rows", X_HOP[2])
    g = send(sx, "rows", Y_LOW)
    scales = (
        1.0 / math.sqrt(all_words * all_offsets),
        1.0 / math.sqrt(all_contexts * all_offsets),
        1.0 / math.sqrt(all_words * all_contexts),
    )
    grad_context, grad_word, grad_offset = whole_call(
        functools.partial(last_sum, scales),
        [(rank, block), (rank, words), (offsets, rank)],
        "last_sum", kx, g, ky, f1, f2, f3, word, other_word,
    )
    return (grad_word, grad_context, grad_offset.T)


def solution(mesh):
    return jax.shard_map(
        per_device,
        mesh=mesh,
        in_specs=(
            P("rows", "section", "cols"),
            P("rows", ("cols", "section")),
            P(None, "rows"),
            P(None, "cols"),
            P(None, "section"),
        ),
        out_specs=(P(None, "rows"), P(None, ("cols", "section", "rows")), P(None, "section")),
        check_vma=False,
    )
```

```python
import functools
import math

import jax
import jax.numpy as jnp
from jax import lax
from jax.experimental import pallas as pl
from jax.experimental.pallas import tpu as pltpu
from jax.sharding import PartitionSpec as P

F32 = jnp.float32
BF16 = jnp.bfloat16
MIB = 1024 * 1024
BIG = 50 * MIB
OWN = 50 * MIB
WORD = 54 * MIB
FRONT_TILE = 1024
TOP = 128
NT = (((1,), (1,)), ((), ()))
TN = (((0,), (0,)), ((), ()))


def dot(a, b):
    return jnp.dot(a, b, preferred_element_type=F32)


def dot_nt(a, b):
    return lax.dot_general(a, b, NT, preferred_element_type=F32)


def dot_tn(a, b):
    return lax.dot_general(a, b, TN, preferred_element_type=F32)


def split_two(v):
    hi = v.astype(BF16)
    return hi, (v - hi.astype(F32)).astype(BF16)


def split_diagonal(v):
    n = v.shape[0]
    hi = v.astype(BF16)
    row = lax.broadcasted_iota(jnp.int32, (n, n), 0)
    col = lax.broadcasted_iota(jnp.int32, (n, n), 1)
    rest = jnp.where(row == col, v - hi.astype(F32), 0.0)
    return hi, jnp.sum(rest, axis=1, keepdims=True)


def square(parts):
    left, corner = parts
    right = jnp.concatenate([left[left.shape[1] :].T, corner], axis=0)
    return jnp.concatenate([left, right], axis=1)


def chunk_count(rank):
    return -(-rank // 128)


def word_spread(words, offsets):
    n = words * offsets
    col = lax.broadcasted_iota(jnp.int32, (words, n), 1)
    row = lax.broadcasted_iota(jnp.int32, (words, n), 0)
    inside = (col >= row * offsets) & (col < row * offsets + offsets)
    return jnp.where(inside, 1.0, 0.0).astype(BF16)


def offset_spread(words, offsets):
    n = words * offsets
    col = lax.broadcasted_iota(jnp.int32, (offsets, n), 1)
    row = lax.broadcasted_iota(jnp.int32, (offsets, n), 0)
    return jnp.where(lax.rem(col, offsets) == row, 1.0, 0.0).astype(BF16)


def start_loads(plan):
    steps = []
    for parts in plan:
        copies = [pltpu.make_async_copy(*p) for p in parts]
        for c in copies:
            c.start()
        steps.append(copies)
    return steps


def position():
    row = lax.axis_index("rows")
    return lax.axis_index("section"), lax.div(row, 2), lax.rem(row, 2)


def front_kernel(pos, word_ref, off_ref, data_ref, ctx_ref, mat_ref, *refs):
    ctx_out, out_ref, d_buf, c_buf, m_buf, d_sem, c_sem, m_sem = refs
    steps, _, tile = d_buf.shape
    words, offsets = word_ref.shape[1], off_ref.shape[0]
    rank = word_ref.shape[0]
    section = pos[0]
    half = steps // 2
    plan = []
    for i in range(steps):
        side = 1 - section if i < half else section
        at = lanes((side * half + i % half) * tile, tile)
        plan.append([(ctx_ref.at[:, at], c_buf.at[i], c_sem.at[i]), (data_ref.at[:, at], d_buf.at[i], d_sem.at[i])])
        if i >= half:
            k = i - half
            plan[-1].append((mat_ref.at[:, pl.ds(k * tile, tile)], m_buf.at[k], m_sem.at[k]))
    loads = start_loads(plan)
    w = word_ref[...]
    o = off_ref[...]
    spread_w = word_spread(words, offsets)
    spread_o = offset_spread(words, offsets)
    wide_w = dot(w, spread_w)
    wide_o = dot_tn(o, spread_o)
    a = (wide_w * wide_o).astype(BF16)
    gram_w = dot_nt(w, w)
    gram_o = dot_tn(o, o)
    m_hi, m_rest = split_diagonal(gram_w * gram_o)
    b = m = own = other = None

    def plus(total, term):
        if total is None:
            return term
        if isinstance(term, tuple):
            return tuple(t + u for t, u in zip(total, term))
        return total + term

    for i in range(steps):
        for c in loads[i]:
            c.wait()
        c = c_buf[i]
        gram = (dot_nt(c, c[:256]), dot_nt(c[256:], c[256:]))
        if i < half:
            ctx_out[:, pl.ds(i * tile, tile)] = dot(m_hi, c) - dot(a, d_buf[i]) + m_rest * c.astype(F32)
            other = plus(other, gram)
        else:
            m = plus(m, dot_nt(c, m_buf[i - half]))
            own = plus(own, gram)
        b = plus(b, dot_nt(c, d_buf[i]))

    own = square(own)
    both = own + square(other)
    n_hi, n_lo = split_two(gram_o * both + own)
    b_hi, b_lo = split_two(b * wide_o)
    total = dot(n_hi, w) + dot(n_lo, w) - m
    total = total - dot_nt(b_hi, spread_w) - dot_nt(b_lo, spread_w)
    low = out_ref.shape[0] - chunk_count(rank) * offsets
    out_ref[pl.ds(0, rank), :] = total
    out_ref[pl.ds(rank, low - rank), :] = jnp.zeros((low - rank, words), F32)
    p_hi, p_lo = split_two(gram_w * both)
    v_hi, v_lo = split_two(b * wide_w)
    off = dot_nt(p_hi, o) + dot_nt(p_lo, o) - dot_nt(v_hi, spread_o) - dot_nt(v_lo, spread_o)
    off = off.T
    for k in range(chunk_count(rank)):
        part = min(128, rank - k * 128)
        at = pl.ds(low + k * offsets, offsets)
        out_ref[at, :] = jnp.zeros((offsets, 128), F32)
        out_ref[at, pl.ds(0, part)] = off[:, k * 128 : k * 128 + part]


def front_part(data, matrix, word, off_t, ctx):
    rank, words = word.shape
    offsets = off_t.shape[0]
    rows, width = data.shape
    tile = min(FRONT_TILE, width // 2)
    steps = width // tile
    half = steps // 2
    out_rows = -(-rank // 8) * 8 + chunk_count(rank) * offsets
    vmem = pl.BlockSpec(memory_space=pltpu.VMEM)
    anywhere = pl.BlockSpec(memory_space=pl.ANY)
    return pl.pallas_call(
        lambda *refs: front_kernel(position(), *refs),
        out_shape=[
            jax.ShapeDtypeStruct((rank, width // 2), F32),
            jax.ShapeDtypeStruct((out_rows, words), F32),
        ],
        in_specs=[vmem, vmem] + [anywhere] * 3,
        out_specs=[vmem] * 2,
        scratch_shapes=[
            pltpu.VMEM((steps, rows, tile), BF16),
            pltpu.VMEM((steps, rank, tile), BF16),
            pltpu.VMEM((half, words, tile), BF16),
            pltpu.SemaphoreType.DMA((steps,)),
            pltpu.SemaphoreType.DMA((steps,)),
            pltpu.SemaphoreType.DMA((half,)),
        ],
        compiler_params=pltpu.CompilerParams(vmem_limit_bytes=WORD),
        cost_estimate=pl.CostEstimate(
            flops=3 * rank * width * (rows + rank), bytes_accessed=rows * width * 2 + rank * width * 2, transcendentals=0
        ),
        name="front",
    )(word, off_t, data, ctx, matrix)


def own_kernel(pos, word_ref, off_ref, data_ref, ctx_ref, mat_ref, after_ref, out_ref, *refs):
    del after_ref
    d_buf, c_buf, m_buf, d_sem, c_sem, m_sem = refs
    steps, _, tile = d_buf.shape
    base = pos[0] * (steps * tile)
    plan = []
    for i in range(steps):
        here = pl.ds(i * tile, tile)
        there = lanes(base + i * tile, tile)
        plan.append([
            (ctx_ref.at[:, there], c_buf.at[i], c_sem.at[i]),
            (mat_ref.at[:, here], m_buf.at[i], m_sem.at[i]),
            (data_ref.at[:, there], d_buf.at[i], d_sem.at[i]),
        ])
    loads = start_loads(plan)
    w = word_ref[...]
    o = off_ref[...]
    words, offsets = w.shape[1], o.shape[0]
    a = (dot(w, word_spread(words, offsets)) * dot_tn(o, offset_spread(words, offsets))).astype(BF16)
    hi, rest = split_diagonal(dot_nt(w, w) * (dot_tn(o, o) + 1.0))
    for i in range(steps):
        for c in loads[i]:
            c.wait()
        c = c_buf[i]
        total = dot(hi, c) - dot(w, m_buf[i]) - dot(a, d_buf[i]) + rest * c.astype(F32)
        out_ref[:, pl.ds(i * tile, tile)] = total


def own_part(data, matrix, word, off_t, ctx, after):
    rank, words = word.shape
    rows, width = data.shape
    half = width // 2
    tile = min(512, half)
    steps = half // tile
    vmem = pl.BlockSpec(memory_space=pltpu.VMEM)
    anywhere = pl.BlockSpec(memory_space=pl.ANY)
    flops = 20 * rank * half * (rows + 2 * rank)
    return pl.pallas_call(
        lambda *refs: own_kernel(position(), *refs),
        out_shape=jax.ShapeDtypeStruct((rank, half), F32),
        in_specs=[vmem, vmem] + [anywhere] * 4,
        out_specs=vmem,
        scratch_shapes=[
            pltpu.VMEM((steps, rows, tile), BF16),
            pltpu.VMEM((steps, rank, tile), BF16),
            pltpu.VMEM((steps, words, tile), BF16),
        ]
        + [pltpu.SemaphoreType.DMA((steps,))] * 3,
        compiler_params=pltpu.CompilerParams(vmem_limit_bytes=OWN),
        cost_estimate=pl.CostEstimate(flops=flops, bytes_accessed=rows * half * 20 + rank * half * 60, transcendentals=0),
        name="own_half",
    )(word, off_t, data, ctx, matrix, after)


def whole_call(kernel, outs, name, *args, after=()):
    vmem = pl.BlockSpec(memory_space=pltpu.VMEM)
    anywhere = pl.BlockSpec(memory_space=pl.ANY)
    n = len(args)

    def body(*refs):
        kernel(position(), *refs[:n], *refs[n + len(after) :])

    return pl.pallas_call(
        body,
        out_shape=[jax.ShapeDtypeStruct(o, F32) for o in outs],
        in_specs=[vmem] * len(args) + [anywhere] * len(after),
        out_specs=[vmem] * len(outs),
        compiler_params=pltpu.CompilerParams(vmem_limit_bytes=24 * MIB),
        cost_estimate=pl.CostEstimate(flops=1024, bytes_accessed=1024, transcendentals=0),
        name=name,
    )(*args, *after)


def lanes(start, width):
    return pl.ds(pl.multiple_of(start, 128), width)


def first_sum(pos, own_ref, got_ref, part_ref, more_ref, x1_ref, x2_ref, x3_ref, y_ref, kx_ref, ky_ref, sum_ref):
    x, y = pos[1], pos[2]
    top, width = kx_ref.shape
    low, span = ky_ref.shape
    block = span // 4
    for hop, ref in ((1, x1_ref), (3, x3_ref), (2, x2_ref), (0, kx_ref)):
        at = lanes(lax.rem(x + hop, 4) * width, width)
        ref[...] = own_ref[pl.ds(0, top), at] + got_ref[pl.ds(0, top), at]
    for side, ref in ((1 - y, y_ref), (y, ky_ref)):
        for k in range(4):
            at = lanes((2 * k + side) * block, block)
            ref[:, pl.ds(k * block, block)] = own_ref[pl.ds(top, low), at] + got_ref[pl.ds(top, low), at]
    sum_ref[...] = part_ref[...] + more_ref[...]


def middle_sum(pos, k_ref, a_ref, b_ref, c_ref, l_ref, g_ref, off_ref, more_ref, *refs):
    sx_ref, kx_ref, x1_ref, x2_ref, x3_ref, ky_ref = refs
    x, y = pos[1], pos[2]
    block = sx_ref.shape[1]
    low = l_ref.shape[0]
    for hop, ref in ((1, x1_ref), (3, x3_ref), (2, x2_ref), (0, ky_ref)):
        at = lanes(lax.rem(x + hop, 4) * block, block)
        ref[pl.ds(0, low), :] = l_ref[:, at] + g_ref[:, at]
    begin = -(-low // 8) * 8
    extra = ky_ref.shape[0] - begin
    total = off_ref[...] + more_ref[...]
    for ref in (x1_ref, x2_ref, x3_ref, ky_ref):
        if begin > low:
            ref[pl.ds(low, begin - low), :] = jnp.zeros((begin - low, block), F32)
        ref[pl.ds(begin, extra), pl.ds(0, 128)] = total
        ref[pl.ds(begin, extra), pl.ds(128, block - 128)] = jnp.zeros((extra, block - 128), F32)
    for side, ref in ((1 - y, sx_ref), (y, kx_ref)):
        at = lanes(side * block, block)
        ref[...] = (k_ref[:, at] + a_ref[:, at]) + (b_ref[:, at] + c_ref[:, at])


def last_sum(scales, pos, k_ref, a_ref, l_ref, b_ref, c_ref, d_ref, w_ref, v_ref, ctx_ref, word_ref, off_ref):
    top = k_ref.shape[0]
    rank = ctx_ref.shape[0]
    low = rank - top
    ctx_ref[pl.ds(0, top), :] = (k_ref[...] + a_ref[...]) * scales[0]
    rows = pl.ds(0, low)
    ctx_ref[pl.ds(top, low), :] = ((l_ref[rows, :] + c_ref[rows, :]) + (b_ref[rows, :] + d_ref[rows, :])) * scales[0]
    word_ref[...] = (w_ref[pl.ds(0, rank), :] + v_ref[pl.ds(0, rank), :]) * scales[1]
    end = -(-low // 8) * 8
    offsets = off_ref.shape[0]
    for k in range(chunk_count(rank)):
        at = pl.ds(end + k * offsets, offsets)
        part = min(128, rank - k * 128)
        total = (l_ref[at, :] + c_ref[at, :]) + (b_ref[at, :] + d_ref[at, :])
        off_ref[:, pl.ds(k * 128, part)] = total[:, :part] * scales[2]


def rows_perm(move):
    pairs = []
    for x in range(4):
        for y in range(2):
            nx, ny = move(x, y)
            pairs.append((x * 2 + y, (nx % 4) * 2 + ny % 2))
    return pairs


def cols_perm(move):
    pairs = []
    for y in range(2):
        for z in range(4):
            ny, nz = move(y, z)
            pairs.append((y * 4 + z, (ny % 2) * 4 + nz % 4))
    return pairs


X_HOP = {h: rows_perm(lambda x, y, h=h: (x + h, y)) for h in (1, 2, 3)}
Y_LOW = rows_perm(lambda x, y: (x, 1 - y))
Z_PAIR = [cols_perm(lambda y, z, h=h: (y, z ^ h)) for h in (1, 2)]
Y_HIGH = cols_perm(lambda y, z: (1 - y, z))
SWAP = [(0, 1), (1, 0)]


def send(v, axis, perm):
    return lax.ppermute(v, axis, perm)


def per_device(tensor_data, matrix_data, word_factor, context_factor, offset_factor):
    words, offsets, width = tensor_data.shape
    rank = word_factor.shape[0]
    all_words = words * lax.axis_size("rows")
    all_offsets = offsets * lax.axis_size("section")
    all_contexts = width * lax.axis_size("cols")
    data = tensor_data.reshape(words * offsets, width)
    off_t = offset_factor.T
    other, part = front_part(data, matrix_data, word_factor, off_t, context_factor)
    got = send(other, "section", SWAP)
    more = send(part, "cols", Y_HIGH)
    own = own_part(data, matrix_data, word_factor, off_t, context_factor, other)

    top = TOP
    low = rank - top
    block = width // 16
    extra = chunk_count(rank) * offsets
    x1, x2, x3, y1, kx, ky, part = whole_call(
        first_sum, [(top, 2 * block)] * 3 + [(low, 4 * block), (top, 2 * block), (low, 4 * block), part.shape],
        "first_sum", own, got, part, more,
    )
    f1 = send(x1, "rows", X_HOP[1])
    f3 = send(x3, "rows", X_HOP[3])
    g = send(y1, "rows", Y_LOW)
    f2 = send(x2, "rows", X_HOP[2])
    part = part + send(part, "cols", Z_PAIR[0])
    word = part + send(part, "cols", Z_PAIR[1])
    off = word[word.shape[0] - extra :]
    more = send(off, "rows", Y_LOW)
    other_word = send(word, "section", SWAP)
    longer = (-(-low // 8) * 8 + extra, block)
    sx, kx, x1, x2, x3, ky = whole_call(
        middle_sum, [(top, block)] * 2 + [longer] * 4, "middle_sum", kx, f1, f2, f3, ky, g, off, more
    )
    f1 = send(x1, "rows", X_HOP[1])
    f3 = send(x3, "rows", X_HOP[3])
    f2 = send(x2, "rows", X_HOP[2])
    g = send(sx, "rows", Y_LOW)
    scales = (
        1.0 / math.sqrt(all_words * all_offsets),
        1.0 / math.sqrt(all_contexts * all_offsets),
        1.0 / math.sqrt(all_words * all_contexts),
    )
    grad_context, grad_word, grad_offset = whole_call(
        functools.partial(last_sum, scales),
        [(rank, block), (rank, words), (offsets, rank)],
        "last_sum", kx, g, ky, f1, f2, f3, word, other_word,
    )
    return (grad_word, grad_context, grad_offset.T)


def solution(mesh):
    return jax.shard_map(
        per_device,
        mesh=mesh,
        in_specs=(
            P("rows", "section", "cols"),
            P("rows", ("cols", "section")),
            P(None, "rows"),
            P(None, "cols"),
            P(None, "section"),
        ),
        out_specs=(P(None, "rows"), P(None, ("cols", "section", "rows")), P(None, "section")),
        check_vma=False,
    )
```
